32 devices in a mesh: replica: 8 (over y, x, core), tensor: 4 (over z).
Axes of the slice: x: 2, y: 2, z: 4, core: 2. Of those that a mesh axis runs over, the one named last changes fastest.
Arguments:
- train_hidden: bfloat16 [1024, 14784], P(None, 'replica'), may hold values from -6 to 6
- out_grad: bfloat16 [1024, 4096], P('tensor'), may hold values from -6 to 6
- master: float32 [14784, 4096], P('replica', 'tensor'), may hold values from -0.046875 to 0.046875
- first_moment: float32 [14784, 4096], P('replica', 'tensor'), may hold values from -6 to 6
- second_moment: float32 [14784, 4096], P('replica', 'tensor'), may hold values from 0.25 to 4
- decode_hidden: bfloat16 [2048, 14784], P('replica'), may hold values from -6 to 6
Outputs:
- new_master: float32 [14784, 4096], P('replica', 'tensor')
- new_first: float32 [14784, 4096], P('replica', 'tensor')
- new_second: float32 [14784, 4096], P('replica', 'tensor')
- decoded: bfloat16 [2048, 4096], P('replica', 'tensor')
The draws below stay inside these ranges and needn't reach their ends.
All inputs are finite; a program needn't handle non-finite values.
Results may differ from the reference program's by a relative error of at most 0.0049.
Values may be sent and summed in bfloat16 or wider, within the bound.
No kernel may reach another device: no remote copies, remote signals or barrier semaphores. Data moves between devices by JAX's collectives and lax.ppermute only.
A program may use at most 128 MiB of HBM per device.

```python
import math
import jax
import jax.numpy as jnp
from jax import lax

D = 4096
FF = 14784
TOK = 1024
ROWS_ALL = 2048


def block_levels(stream_key, dims, shards, smallest, largest):
    factor_of = 1.0
    for axis_at, shards_of in shards:
        draws = jax.random.uniform(jax.random.fold_in(jax.random.fold_in(stream_key, 6), axis_at), (shards_of,), jnp.float32, smallest / len(shards), largest / len(shards))
        factor_of = factor_of * jnp.repeat(jnp.exp(draws), dims[axis_at] // shards_of).reshape((-1,) + (1,) * (len(dims) - 1 - axis_at))
    return factor_of


def noise(stream_key, dims, deviation, reach, shards=(), dtype=jnp.bfloat16):
    array = deviation * jax.random.normal(stream_key, dims, jnp.float32)
    if shards:
        array = array * block_levels(stream_key, dims, shards, -0.22, 0.18)
    return jnp.clip(array, -reach, reach).astype(dtype)


def setup_inputs(seed: int = 0) -> dict:
    streams_of = jax.random.split(jax.random.key(seed), 7)
    return {
        "train_hidden": noise(streams_of[0], (TOK, FF), 1.0, 6.0, ((1, 8),)),
        "out_grad": noise(streams_of[1], (TOK, D), 1.0, 6.0, ((0, 4),)),
        "master": noise(streams_of[2], (FF, D), FF ** -0.5, 0.046875, ((0, 8), (1, 4)), jnp.float32),
        "first_moment": noise(streams_of[3], (FF, D), 1.0, 6.0, ((0, 8), (1, 4)), jnp.float32),
        "second_moment": jnp.clip(jnp.exp(math.log(4.0) - 2.7725887 * jax.random.uniform(streams_of[4], (FF, D), jnp.float32) ** block_levels(streams_of[4], (FF, D), ((0, 8), (1, 4)), -0.2, 0.2)), 0.25, 4.0),
        "decode_hidden": noise(streams_of[5], (ROWS_ALL, FF), 1.0, 6.0, ((0, 8),)),
    }


def reference(train_hidden, out_grad, master, first_moment, second_moment, decode_hidden):
    grad = lax.dot_general(train_hidden, out_grad, (((0,), (0,)), ((), ())), preferred_element_type=jnp.float32)
    grad = grad * (1.0 / math.sqrt(TOK))
    new_first = 0.9 * first_moment + 0.1 * grad
    new_second = 0.95 * second_moment + 0.05 * grad * grad
    new_master = master - 0.002 * new_first / (jnp.sqrt(new_second) + 1e-08)
    weights = new_master.astype(jnp.bfloat16)
    decoded = jnp.dot(decode_hidden, weights, preferred_element_type=jnp.float32).astype(jnp.bfloat16)
    return (new_master, new_first, new_second, decoded)
```

```python
import math

import jax
import jax.numpy as jnp
from jax import lax
from jax.sharding import PartitionSpec as P


def xor_permute(array, axis, size, mask):
    return lax.ppermute(array, axis, [(i, i ^ mask) for i in range(size)])


def gather_columns(out_grad, devices, planes):
    mine = lax.axis_index("tensor")
    half = lax.rem(lax.axis_index("replica"), 2)
    tokens, width = out_grad.shape[0], out_grad.shape[1] // planes
    own = lax.dynamic_slice(out_grad, (0, mine * width), (tokens, width))
    pieces = []
    for mask in range(1, planes):
        block = lax.dynamic_slice(
            out_grad, (half * (tokens // 2), (mine ^ mask) * width), (tokens // 2, width)
        )
        pieces.append(xor_permute(block, "tensor", planes, mask))
    fetched = jnp.stack(pieces)
    other = xor_permute(fetched, "replica", devices, 1)
    both = jnp.where(
        half == 0,
        jnp.concatenate([fetched, other], axis=1),
        jnp.concatenate([other, fetched], axis=1),
    )
    stacked = jnp.concatenate([own[None], both], axis=0)
    ordered = [
        lax.dynamic_index_in_dim(stacked, mine ^ plane, 0, keepdims=False)
        for plane in range(planes)
    ]
    return jnp.concatenate(ordered, axis=0)


def per_device(train_hidden, out_grad, master, first_moment, second_moment, decode_hidden):
    devices, planes = lax.axis_size("replica"), lax.axis_size("tensor")
    chips = devices // 2
    chip = lax.axis_index("replica") // 2
    parity = lax.rem(lax.axis_index("tensor"), 2)
    tokens_all = train_hidden.shape[0]
    rows, hidden = decode_hidden.shape
    block = hidden // chips

    windows = jnp.stack(
        [decode_hidden[:, k * block : (k + 1) * block] for k in range(chips)]
    )

    def part(mask, start, count):
        return lax.dynamic_slice(windows, (chip ^ mask, start, 0), (1, count, block))[0]

    columns = gather_columns(out_grad, devices, planes)

    held = {}
    order = sorted(range(1, chips), key=lambda m: -m.bit_count())
    for mask in order:
        direct = 0 if mask.bit_count() > 1 else rows // 2
        shared = (rows - direct) // 2
        pieces = []
        if direct:
            sent = part(mask, 0, direct)
            pieces.append(xor_permute(sent, "replica", devices, 2 * mask))
        sent = part(mask, direct + parity * shared, shared)
        mine = xor_permute(sent, "replica", devices, 2 * mask)
        pieces.append(mine)
        pieces.append(xor_permute(mine, "tensor", planes, 1))
        held[mask] = (direct, shared, jnp.concatenate(pieces, axis=0))

    grad = lax.dot_general(
        train_hidden, columns, (((0,), (0,)), ((), ())), preferred_element_type=jnp.float32
    )
    grad = grad * (1.0 / math.sqrt(tokens_all))
    new_first = 0.9 * first_moment + 0.1 * grad
    new_second = 0.95 * second_moment + 0.05 * grad * grad
    new_master = master - 0.002 * new_first / (jnp.sqrt(new_second) + 1e-08)
    weights = new_master.astype(jnp.bfloat16)

    swapped = xor_permute(weights, "replica", devices, 1)
    first = lax.rem(lax.axis_index("replica"), 2) == 0
    pair = jnp.concatenate(
        [jnp.where(first, weights, swapped), jnp.where(first, swapped, weights)], axis=0
    )

    def partial(held_rows):
        return jnp.dot(held_rows, pair, preferred_element_type=jnp.float32)

    total = partial(part(0, 0, rows))
    for mask in order:
        direct, shared, held_rows = held[mask]
        sums = partial(held_rows).astype(jnp.bfloat16)
        back = xor_permute(sums, "replica", devices, 2 * mask).astype(jnp.float32)
        low, high = back[direct : direct + shared], back[direct + shared :]
        low, high = jnp.where(parity == 0, low, high), jnp.where(parity == 0, high, low)
        total = total + jnp.concatenate([back[:direct], low, high], axis=0)
    return (new_master, new_first, new_second, total.astype(jnp.bfloat16))


def solution(mesh):
    placed = (
        P(None, "replica"),
        P("tensor", None),
        P("replica", "tensor"),
        P("replica", "tensor"),
        P("replica", "tensor"),
        P("replica", None),
    )
    return jax.shard_map(
        per_device,
        mesh=mesh,
        in_specs=placed,
        out_specs=(
            P("replica", "tensor"),
            P("replica", "tensor"),
            P("replica", "tensor"),
            P("replica", "tensor"),
        ),
        check_vma=False,
    )
```

```python
import functools
import math

import jax
import jax.numpy as jnp
from jax import lax
from jax.experimental import pallas as pl
from jax.experimental.pallas import tpu as pltpu
from jax.sharding import PartitionSpec as P

OVER_FIRST = (((0,), (0,)), ((), ()))


def xor_permute(array, axis, size, mask):
    return lax.ppermute(array, axis, [(i, i ^ mask) for i in range(size)])


def adam_kernel(planes, scale, waits, place_ref, hidden_ref, own_ref, fetched_ref, swapped_ref, *refs):
    master_ref, first_ref, second_ref = refs[:3]
    new_master_ref, new_first_ref, new_second_ref, weights_ref, columns_ref = refs[3 + waits :]
    tokens = own_ref.shape[0]
    half = tokens // 2

    @pl.when(pl.program_id(0) == 0)
    def _():
        plane, core = place_ref[0], place_ref[1]
        columns_ref[pl.ds(pl.multiple_of(plane * tokens, tokens), tokens), :] = own_ref[...]
        for mask in range(1, planes):
            start = (plane ^ mask) * tokens
            mine = pl.multiple_of(start + core * half, half)
            other = pl.multiple_of(start + (1 - core) * half, half)
            columns_ref[pl.ds(mine, half), :] = fetched_ref[mask - 1]
            columns_ref[pl.ds(other, half), :] = swapped_ref[mask - 1]

    grad = jnp.dot(hidden_ref[...], columns_ref[...], preferred_element_type=jnp.float32)
    grad = grad * scale
    new_first = 0.9 * first_ref[...] + 0.1 * grad
    new_second = 0.95 * second_ref[...] + 0.05 * grad * grad
    new_master = master_ref[...] - 0.002 * new_first / (jnp.sqrt(new_second) + 1e-08)
    new_master_ref[...] = new_master
    new_first_ref[...] = new_first
    new_second_ref[...] = new_second
    weights_ref[...] = new_master.astype(jnp.bfloat16)


def adam(place, planes, hidden, out_grad, fetched, swapped, state, step, blocks, before, after):
    rows, tokens_all = hidden.shape
    width = state[0].shape[1]
    tokens = tokens_all // planes
    start, stop = blocks
    block = pl.BlockSpec((step, width), lambda i, s: (i + start, 0))
    whole = pl.BlockSpec(fetched.shape, lambda i, s: (0, 0, 0))
    full = jax.ShapeDtypeStruct((rows, width), jnp.float32)
    waits = len(before) + len(after)
    size = (stop - start) * step * width
    return pl.pallas_call(
        functools.partial(adam_kernel, planes, 1.0 / math.sqrt(tokens_all), waits),
        out_shape=[full] * 3 + [jax.ShapeDtypeStruct((rows, width), jnp.bfloat16)],
        grid_spec=pltpu.PrefetchScalarGridSpec(
            num_scalar_prefetch=1,
            grid=(stop - start,),
            in_specs=[
                pl.BlockSpec((step, tokens_all), lambda i, s: (i + start, 0)),
                pl.BlockSpec((tokens, width), lambda i, s: (0, s[0])),
                whole,
                whole,
                block,
                block,
                block,
            ]
            + [pl.BlockSpec(memory_space=pl.ANY)] * waits,
            out_specs=[block] * 4,
            scratch_shapes=[pltpu.VMEM((tokens_all, width), jnp.bfloat16)],
        ),
        input_output_aliases={8 + i: i for i in range(len(before))},
        compiler_params=pltpu.CompilerParams(vmem_limit_bytes=40 * 1024 * 1024),
        cost_estimate=pl.CostEstimate(
            flops=2 * size * tokens_all, bytes_accessed=28 * size, transcendentals=2 * size
        ),
    )(place, hidden, out_grad, fetched, swapped, *state, *before, *after)


def per_device(train_hidden, out_grad, master, first_moment, second_moment, decode_hidden):
    devices, planes = lax.axis_size("replica"), lax.axis_size("tensor")
    chips = devices // 2
    plane, device = lax.axis_index("tensor"), lax.axis_index("replica")
    chip, core = lax.div(device, 2), lax.rem(device, 2)
    parity = lax.rem(plane, 2)
    even = parity == 0
    tokens, width = out_grad.shape[0], out_grad.shape[1] // planes
    rows, hidden = decode_hidden.shape
    block = hidden // devices
    cut = block // 2 // 8 * 8

    pieces = []
    for mask in range(1, planes):
        part = lax.dynamic_slice(
            out_grad,
            (core * (tokens // 2), (plane ^ mask) * width),
            (tokens // 2, width),
        )
        pieces.append(xor_permute(part, "tensor", planes, mask))

    windows = decode_hidden.T.reshape(chips, 2, block, rows)

    def part(mask, to_core, low, high):
        return lax.dynamic_slice(
            windows, (chip ^ mask, to_core, low, 0), (1, 1, high - low, rows)
        ).reshape(high - low, rows)

    def to_peer(array, mask, cross):
        return xor_permute(array, "replica", devices, 2 * mask + cross)

    def to_peer_by_plane(array, mask):
        pairs = [
            (r * planes + z, (r ^ (2 * mask + z % 2)) * planes + z)
            for r in range(devices)
            for z in range(planes)
        ]
        return lax.ppermute(array, ("replica", "tensor"), pairs)

    order = sorted(range(1, chips), key=lambda m: -m.bit_count())
    far = [mask for mask in order if mask.bit_count() > 1]
    near = [mask for mask in order if mask.bit_count() == 1]
    shared, straight = {}, {}
    for mask in far:
        shared[mask] = to_peer_by_plane(part(mask, core ^ parity, 0, block), mask)
    for mask in near:
        shared[mask] = to_peer_by_plane(part(mask, core ^ parity, 0, cut), mask)
    for mask in near:
        straight[mask] = [
            to_peer(part(mask, core, cut, block), mask, 0),
            to_peer(part(mask, 1 - core, cut, block), mask, 1),
        ]
    passed = {mask: xor_permute(shared[mask], "tensor", planes, 1) for mask in order}
    beside = xor_permute(part(0, 1 - core, 0, block), "replica", devices, 1)

    fetched = jnp.stack(pieces)
    swapped = xor_permute(fetched, "replica", devices, 1)
    place = jnp.stack([plane, core]).astype(jnp.int32)
    state = (master, first_moment, second_moment)
    step = 320 if master.shape[0] > 320 else master.shape[0]
    blocks = pl.cdiv(master.shape[0], step)
    middle = (blocks + 1) // 2
    common = (place, planes, train_hidden.T, out_grad, fetched, swapped, state, step)
    out = adam(*common, (0, middle), (), [shared[mask] for mask in far])
    if middle < blocks:
        out = adam(*common, (middle, blocks), out, [shared[mask] for mask in near])
    new_master, new_first, new_second, weights = out

    def times_weights(held):
        return lax.dot_general(held, weights, OVER_FIRST, preferred_element_type=jnp.float32)

    def partial(mask):
        if mask == 0:
            keep, give = [part(0, core, 0, block)], [beside]
        else:
            keep = [jnp.where(even, shared[mask], passed[mask])]
            give = [jnp.where(even, passed[mask], shared[mask])]
        if mask in straight:
            keep.append(straight[mask][0])
            give.append(straight[mask][1])
        given = times_weights(jnp.concatenate(give, axis=0))
        kept = times_weights(jnp.concatenate(keep, axis=0))
        return kept + xor_permute(given, "replica", devices, 1)

    total = partial(0)
    for mask in order:
        sums = partial(mask).astype(jnp.bfloat16)
        total = total + to_peer(sums, mask, 0).astype(jnp.float32)
    return (new_master, new_first, new_second, total.astype(jnp.bfloat16))


def solution(mesh):
    placed = (
        P(None, "replica"),
        P("tensor", None),
        P("replica", "tensor"),
        P("replica", "tensor"),
        P("replica", "tensor"),
        P("replica", None),
    )
    return jax.shard_map(
        per_device,
        mesh=mesh,
        in_specs=placed,
        out_specs=(
            P("replica", "tensor"),
            P("replica", "tensor"),
            P("replica", "tensor"),
            P("replica", "tensor"),
        ),
        check_vma=False,
    )
```

```python
import functools
import math

import jax
import jax.numpy as jnp
from jax import lax
from jax.experimental import pallas as pl
from jax.experimental.pallas import tpu as pltpu
from jax.sharding import PartitionSpec as P

FREE = pl.CostEstimate(flops=0, bytes_accessed=0, transcendentals=0)
OVER_FIRST = (((0,), (0,)), ((), ()))


def xor_permute(array, axis, size, mask):
    return lax.ppermute(array, axis, [(i, i ^ mask) for i in range(size)])


def adam_kernel(planes, scale, waits, place_ref, hidden_ref, own_ref, *refs):
    crossed = planes - 1
    fetched_refs, swapped_refs = refs[:crossed], refs[crossed : 2 * crossed]
    master_ref, first_ref, second_ref = refs[2 * crossed : 2 * crossed + 3]
    new_master_ref, new_first_ref, new_second_ref, weights_ref, columns_ref = refs[2 * crossed + 3 + waits :]
    tokens = own_ref.shape[0]
    half = tokens // 2

    @pl.when(pl.program_id(0) == 0)
    def _():
        plane, core = place_ref[0], place_ref[1]
        columns_ref[pl.ds(pl.multiple_of(plane * tokens, tokens), tokens), :] = own_ref[...]
        for mask in range(1, planes):
            start = (plane ^ mask) * tokens
            mine = pl.multiple_of(start + core * half, half)
            other = pl.multiple_of(start + (1 - core) * half, half)
            columns_ref[pl.ds(mine, half), :] = fetched_refs[mask - 1][...]
            columns_ref[pl.ds(other, half), :] = swapped_refs[mask - 1][...]

    grad = jnp.dot(hidden_ref[...], columns_ref[...], preferred_element_type=jnp.float32)
    grad = grad * scale
    new_first = 0.9 * first_ref[...] + 0.1 * grad
    new_second = 0.95 * second_ref[...] + 0.05 * grad * grad
    new_master = master_ref[...] - 0.002 * new_first / (jnp.sqrt(new_second) + 1e-08)
    new_master_ref[...] = new_master
    new_first_ref[...] = new_first
    new_second_ref[...] = new_second
    weights_ref[...] = new_master.astype(jnp.bfloat16)


def adam(place, planes, hidden, out_grad, fetched, swapped, state, step, blocks, before):
    rows, tokens_all = hidden.shape
    width = state[0].shape[1]
    tokens = tokens_all // planes
    start, stop = blocks
    block = pl.BlockSpec((step, width), lambda i, s: (i + start, 0))
    full = pltpu.HBM((rows, width), jnp.float32)
    operands = [hidden, out_grad, *fetched, *swapped, *state, *before]
    operands = [
        x if 2 <= i < 2 * planes else pltpu.with_memory_space_constraint(x, pltpu.HBM)
        for i, x in enumerate(operands)
    ]
    return pl.pallas_call(
        functools.partial(adam_kernel, planes, 1.0 / math.sqrt(tokens_all), len(before)),
        out_shape=[full] * 3 + [pltpu.HBM((rows, width), jnp.bfloat16)],
        grid_spec=pltpu.PrefetchScalarGridSpec(
            num_scalar_prefetch=1,
            grid=(stop - start,),
            in_specs=[
                pl.BlockSpec((step, tokens_all), lambda i, s: (i + start, 0)),
                pl.BlockSpec((tokens, width), lambda i, s: (0, s[0])),
            ]
            + [pl.BlockSpec((tokens // 2, width), lambda i, s: (0, 0))] * (2 * planes - 2)
            + [block] * 3
            + [pl.BlockSpec(memory_space=pl.ANY)] * len(before),
            out_specs=[block] * 4,
            scratch_shapes=[pltpu.VMEM((tokens_all, width), jnp.bfloat16)],
        ),
        input_output_aliases={4 + 2 * planes + i: i for i in range(len(before))},
        compiler_params=pltpu.CompilerParams(vmem_limit_bytes=32 * 1024 * 1024),
        cost_estimate=FREE,
    )(place, *operands)


def product_kernel(crossed, straight, place_ref, *refs):
    held_refs, (own_ref, other_ref), out_refs = refs[: crossed * 2 + straight], refs[-4:-2], refs[-2:]
    parity, core = lax.rem(place_ref[0], 2), place_ref[1]
    cut = held_refs[0].shape[0] if crossed else 0

    def dot(held, weights):
        return lax.dot_general(held, weights, OVER_FIRST, preferred_element_type=jnp.float32)

    def write(first_ref, second_ref):
        total = 0.0
        if crossed:
            total = dot(held_refs[0][...], first_ref[:cut]) + dot(held_refs[1][...], second_ref[:cut])
        if straight:
            total = total + dot(held_refs[-1][core], own_ref[cut:]) + dot(held_refs[-1][1 - core], other_ref[cut:])
        half = out_refs[0].shape[0]
        out_refs[0][...] = total[:half].astype(out_refs[0].dtype)
        out_refs[1][...] = total[half:].astype(out_refs[1].dtype)

    if crossed:
        pl.when(parity == 0)(lambda: write(own_ref, other_ref))
        pl.when(parity != 0)(lambda: write(other_ref, own_ref))
    else:
        write(own_ref, other_ref)


def product(place, crossed, straight, own, other, dtype, cost):
    block, width = own.shape
    columns = min(512, width)
    rows = (crossed or straight)[0].shape[-1]
    weights = pl.BlockSpec((block, columns), lambda j, s: (0, j))
    half = pl.BlockSpec((rows // 2, columns), lambda j, s: (0, j))
    specs = [pl.BlockSpec(array.shape, lambda j, s: (0, 0)) for array in crossed]
    if straight:
        chip = straight[1]
        specs.append(pl.BlockSpec((2, *straight[0].shape[1:]), lambda j, s: (s[2] if chip else 0, 0, 0)))
    return pl.pallas_call(
        functools.partial(product_kernel, bool(crossed), bool(straight)),
        out_shape=[jax.ShapeDtypeStruct((rows // 2, width), dtype)] * 2,
        grid_spec=pltpu.PrefetchScalarGridSpec(
            num_scalar_prefetch=1,
            grid=(width // columns,),
            in_specs=[*specs, weights, weights],
            out_specs=[half, half],
        ),
        compiler_params=pltpu.CompilerParams(vmem_limit_bytes=28 * 1024 * 1024),
        cost_estimate=cost,
    )(place, *crossed, *straight[:1], own, other)


def hold(token, *arrays, flops=10**12):
    anywhere = pl.BlockSpec(memory_space=pl.ANY)
    return pl.pallas_call(
        lambda *refs: None,
        out_shape=jax.ShapeDtypeStruct(token.shape, token.dtype),
        in_specs=[anywhere] * (1 + len(arrays)),
        out_specs=anywhere,
        input_output_aliases={0: 0},
        compiler_params=pltpu.CompilerParams(vmem_limit_bytes=1024 * 1024),
        cost_estimate=pl.CostEstimate(flops=flops, bytes_accessed=0, transcendentals=0),
    )(token, *arrays)


def after(token, arrays):
    return lax.optimization_barrier((token, arrays))


def per_device(train_hidden, out_grad, master, first_moment, second_moment, decode_hidden):
    devices, planes = lax.axis_size("replica"), lax.axis_size("tensor")
    chips = devices // 2
    plane, device = lax.axis_index("tensor"), lax.axis_index("replica")
    chip, core = lax.div(device, 2), lax.rem(device, 2)
    parity = lax.rem(plane, 2)
    rows, hidden = decode_hidden.shape
    block = hidden // devices
    tokens, width = out_grad.shape[0], out_grad.shape[1] // planes
    token = jnp.stack([plane, core, chip]).astype(jnp.int32)

    near = 1
    sides = [mask for mask in range(2, chips) if mask % 2 == 0]
    fars = [mask for mask in range(2, chips) if mask % 2 == 1]

    def to_peer(array, mask, cross=0):
        return xor_permute(array, "replica", devices, 2 * mask + cross)

    windows = decode_hidden.T.reshape(devices, block, rows)

    def part(mask, to_core):
        return lax.dynamic_index_in_dim(windows, (chip ^ mask) * 2 + to_core, 0, keepdims=False)

    far_cuts = [part(mask, core ^ parity) for mask in fars]
    column_cuts = [
        lax.dynamic_slice(
            out_grad,
            (core * (tokens // 2), (plane ^ mask) * width),
            (tokens // 2, width),
        )
        for mask in range(1, planes)
    ]
    shared = {mask: to_peer(cut, mask) for mask, cut in zip(fars, far_cuts, strict=True)}
    pieces = [xor_permute(cut, "tensor", planes, mask + 1) for mask, cut in enumerate(column_cuts)]
    token = hold(token, *far_cuts, *column_cuts)

    cut = block // 2 // 16 * 16

    def straight_part(mask, low):
        return lax.dynamic_slice(windows, ((chip ^ mask) * 2, low, 0), (2, block - low, rows))

    token, windows = after(token, windows)
    near_cut = part(near, core ^ parity)[:cut]
    side_cuts = {mask: straight_part(mask, 0) for mask in sides}
    rest_cut = straight_part(near, cut)
    shared[near] = to_peer(near_cut, near)
    straight = {mask: to_peer(cut, mask) for mask, cut in side_cuts.items()}
    token = hold(token, near_cut, rest_cut, *side_cuts.values())

    passed = {}
    for mask in fars:
        token, shared[mask] = after(token, shared[mask])
        passed[mask] = xor_permute(shared[mask], "tensor", planes, 1)
    token = hold(token, *(shared[mask] for mask in fars))

    token, pieces = after(token, pieces)
    swapped = [to_peer(piece, 0, 1) for piece in pieces]
    state = (master, first_moment, second_moment)
    step = min(320, block)
    blocks = pl.cdiv(block, step)
    middle = (blocks + 1) // 2
    common = (planes, train_hidden.T, out_grad, pieces, swapped, state, step)
    out = list(adam(token, *common, (0, middle), ()))
    shared[near], rest_cut, out[0] = lax.optimization_barrier((shared[near], rest_cut, out[0]))
    straight[near] = to_peer(rest_cut, near)
    passed[near] = xor_permute(shared[near], "tensor", planes, 1)
    if middle < blocks:
        out = adam(token, *common, (middle, blocks), out)
    new_master, new_first, new_second, weights = out

    other = to_peer(weights, 0, 1)
    token = hold(token, *(passed[mask] for mask in fars), flops=2 * 10**9)
    token = hold(token, passed[near], *straight.values(), flops=10**11)

    low = {near: [], **{mask: [] for mask in sides}}
    high = {near: [], **{mask: [] for mask in sides}}
    for mask in fars:
        out = product(token, (shared[mask], passed[mask]), (), weights, other, jnp.bfloat16, FREE)
        low[mask ^ near].append(to_peer(out[0], near))
        high[near].append(to_peer(out[1], mask ^ near))
    back = []
    for mask in (near, *sides):
        crossed = (shared[near], passed[near]) if mask == near else ()
        out = product(token, crossed, (straight[mask], False), weights, other, jnp.float32, FREE)
        sums = [
            functools.reduce(jnp.add, [array.astype(jnp.float32) for array in arrays], mine)
            for mine, arrays in zip(out, (low[mask], high[mask]), strict=True)
        ]
        back.append(to_peer(jnp.concatenate(sums, axis=0).astype(jnp.bfloat16), mask))
    cost = pl.CostEstimate(flops=4 * rows * block * width, bytes_accessed=4 * block * width, transcendentals=0)
    total = product(token, (), (windows, True), weights, other, jnp.float32, cost)
    total = lax.optimization_barrier(jnp.concatenate(total, axis=0))
    for sums in back:
        total = total + sums.astype(jnp.float32)
    decoded = total.astype(jnp.bfloat16)
    return (new_master, new_first, new_second, decoded)


def solution(mesh):
    placed = (
        P(None, "replica"),
        P("tensor", None),
        P("replica", "tensor"),
        P("replica", "tensor"),
        P("replica", "tensor"),
        P("replica", None),
    )
    return jax.shard_map(
        per_device,
        mesh=mesh,
        in_specs=placed,
        out_specs=(
            P("replica", "tensor"),
            P("replica", "tensor"),
            P("replica", "tensor"),
            P("replica", "tensor"),
        ),
        check_vma=False,
    )
```

```python
import functools
import math

import jax
import jax.numpy as jnp
from jax import lax
from jax.experimental import pallas as pl
from jax.experimental.pallas import tpu as pltpu
from jax.sharding import PartitionSpec as P

FREE = pl.CostEstimate(flops=0, bytes_accessed=0, transcendentals=0)
OVER_FIRST = (((0,), (0,)), ((), ()))


def xor_permute(array, axis, size, mask):
    return lax.ppermute(array, axis, [(i, i ^ mask) for i in range(size)])


def cut_kernel(planes, masks, place_ref, windows_ref, out_grad_ref, *refs):
    *target_refs, sems = refs
    plane, core, chip = place_ref[0], place_ref[1], place_ref[2]
    half, width = target_refs[-1].shape
    copies = []
    for mask, target_ref in zip(masks, target_refs):
        device = (chip ^ mask) * 2 + (core ^ lax.rem(plane, 2))
        copies.append(pltpu.make_async_copy(windows_ref.at[device], target_ref, sems.at[len(copies)]))
    for mask, target_ref in zip(range(1, planes), target_refs[len(masks) :]):
        rows = pl.ds(pl.multiple_of(core * half, half), half)
        columns = pl.ds(pl.multiple_of((plane ^ mask) * width, width), width)
        copies.append(pltpu.make_async_copy(out_grad_ref.at[rows, columns], target_ref, sems.at[len(copies)]))
    for copy in copies:
        copy.start()
    for copy in copies:
        copy.wait()


def cut(place, windows, out_grad, planes, masks):
    tokens, width = out_grad.shape[0], out_grad.shape[1] // planes
    anywhere = pl.BlockSpec(memory_space=pl.ANY)
    pieces = len(masks) + planes - 1
    out = pl.pallas_call(
        functools.partial(cut_kernel, planes, masks),
        out_shape=[pltpu.VMEM(windows.shape[1:], windows.dtype)] * len(masks)
        + [pltpu.VMEM((tokens // 2, width), out_grad.dtype)] * (planes - 1),
        in_specs=[pl.BlockSpec(memory_space=pltpu.SMEM), anywhere, anywhere],
        out_specs=[pl.BlockSpec(memory_space=pltpu.VMEM)] * pieces,
        scratch_shapes=[pltpu.SemaphoreType.DMA((pieces,))],
        compiler_params=pltpu.CompilerParams(vmem_limit_bytes=8 * 1024 * 1024),
        cost_estimate=FREE,
    )(place, *[pltpu.with_memory_space_constraint(x, pltpu.HBM) for x in (windows, out_grad)])
    return out[: len(masks)], out[len(masks) :]


def adam_kernel(planes, scale, cuts, waits, place_ref, own_ref, *refs):
    crossed = planes - 1
    fetched_refs, swapped_refs = refs[:crossed], refs[crossed : 2 * crossed]
    hidden_ref, *state_refs = refs[2 * crossed : 2 * crossed + 4]
    *out_refs, weights_ref, columns_ref, rows_ref, held_ref, row_sem, in_sems, out_sems = refs[2 * crossed + 4 + waits :]
    base = cuts[0]
    rows_copy = pltpu.make_async_copy(hidden_ref, rows_ref, row_sem)
    copies_in, copies_out = [], []
    for i, (low, high) in enumerate(zip(cuts, cuts[1:])):
        here, there = slice(low - base, high - base), slice(low, high)
        copies_in.append(
            [
                pltpu.make_async_copy(ref.at[there], held_ref.at[k, here], in_sems.at[i, k])
                for k, ref in enumerate(state_refs)
            ]
        )
        copies_out.append(
            [
                pltpu.make_async_copy(held_ref.at[k, here], ref.at[there], out_sems.at[i, k])
                for k, ref in enumerate(out_refs)
            ]
        )
    rows_copy.start()
    for copies in copies_in[:2]:
        for copy in copies:
            copy.start()

    tokens = own_ref.shape[0]
    half = tokens // 2
    plane, core = place_ref[0], place_ref[1]
    columns_ref[pl.ds(pl.multiple_of(plane * tokens, tokens), tokens), :] = own_ref[...]
    for mask in range(1, planes):
        start = (plane ^ mask) * tokens
        mine = pl.multiple_of(start + core * half, half)
        other = pl.multiple_of(start + (1 - core) * half, half)
        columns_ref[pl.ds(mine, half), :] = fetched_refs[mask - 1][...]
        columns_ref[pl.ds(other, half), :] = swapped_refs[mask - 1][...]

    rows_copy.wait()
    for i, (low, high) in enumerate(zip(cuts, cuts[1:])):
        here = slice(low - base, high - base)
        grad = jnp.dot(rows_ref[here], columns_ref[...], preferred_element_type=jnp.float32)
        grad = grad * scale
        for copy in copies_in[i]:
            copy.wait()
        for copy in copies_in[i + 2] if i + 2 < len(copies_in) else ():
            copy.start()
        new_first = 0.9 * held_ref[1, here] + 0.1 * grad
        new_second = 0.95 * held_ref[2, here] + 0.05 * grad * grad
        new_master = held_ref[0, here] - 0.002 * new_first / (jnp.sqrt(new_second) + 1e-08)
        weights_ref[here] = new_master.astype(jnp.bfloat16)
        for k, new in enumerate((new_master, new_first, new_second)):
            held_ref[k, here] = new
            copies_out[i][k].start()
    for copies in copies_out:
        for copy in copies:
            copy.wait()


def adam(place, planes, hidden, own, fetched, swapped, state, cuts, before):
    count, tokens_all = hidden.shape
    rows, width = state[0].shape
    full = pltpu.HBM((rows, width), jnp.float32)
    inside = pl.BlockSpec(memory_space=pltpu.VMEM)
    outside = pl.BlockSpec(memory_space=pl.ANY)
    near = [own, *fetched, *swapped]
    far = [pltpu.with_memory_space_constraint(x, pltpu.HBM) for x in (hidden, *state, *before)]
    return pl.pallas_call(
        functools.partial(adam_kernel, planes, 1.0 / math.sqrt(tokens_all), cuts, len(before)),
        out_shape=[full] * 3 + [jax.ShapeDtypeStruct((count, width), jnp.bfloat16)],
        in_specs=[pl.BlockSpec(memory_space=pltpu.SMEM)] + [inside] * len(near) + [outside] * len(far),
        out_specs=[outside] * 3 + [inside],
        scratch_shapes=[
            pltpu.VMEM((tokens_all, width), jnp.bfloat16),
            pltpu.VMEM((count, tokens_all), jnp.bfloat16),
            pltpu.VMEM((3, count, width), jnp.float32),
            pltpu.SemaphoreType.DMA,
            pltpu.SemaphoreType.DMA((len(cuts) - 1, 3)),
            pltpu.SemaphoreType.DMA((len(cuts) - 1, 3)),
        ],
        input_output_aliases={1 + len(near) + 4 + i: i for i in range(len(before))},
        compiler_params=pltpu.CompilerParams(vmem_limit_bytes=28 * 1024 * 1024),
        cost_estimate=FREE,
    )(place, *near, *far)


def product_kernel(crossed, parts, place_ref, *refs):
    own_refs, other_refs, out_refs = refs[-2 * parts - 2 : -parts - 2], refs[-parts - 2 : -2], refs[-2:]
    held_refs = refs[: -2 * parts - 2]
    parity, core = lax.rem(place_ref[0], 2), place_ref[1]
    cut = held_refs[0].shape[0] if crossed else 0

    def dot(weights_refs, low, high, read):
        total, at = 0.0, 0
        for ref in weights_refs:
            begin, end = max(low, at), min(high, at + ref.shape[0])
            if begin < end:
                total = total + lax.dot_general(
                    read(begin, end), ref[begin - at : end - at], OVER_FIRST, preferred_element_type=jnp.float32
                )
            at += ref.shape[0]
        return total

    def write(first_refs, second_refs):
        block = sum(ref.shape[0] for ref in own_refs)
        total = 0.0
        if crossed:
            total = dot(first_refs, 0, cut, lambda begin, end: held_refs[0][begin:end])
            total = total + dot(second_refs, 0, cut, lambda begin, end: held_refs[1][begin:end])
        if cut < block:
            straight_ref = held_refs[-1]
            total = total + dot(own_refs, cut, block, lambda begin, end: straight_ref[core, begin - cut : end - cut])
            total = total + dot(
                other_refs, cut, block, lambda begin, end: straight_ref[1 - core, begin - cut : end - cut]
            )
        half = out_refs[0].shape[0]
        out_refs[0][...] = total[:half].astype(out_refs[0].dtype)
        out_refs[1][...] = total[half:].astype(out_refs[1].dtype)

    if crossed:
        pl.when(parity == 0)(lambda: write(own_refs, other_refs))
        pl.when(parity != 0)(lambda: write(other_refs, own_refs))
    else:
        write(own_refs, other_refs)


def product(place, crossed, straight, own, other, dtype, cost):
    width = own[0].shape[1]
    rows = (*crossed, *straight)[0].shape[-1]
    operands = [*crossed, *straight, *own, *other]
    operands = [pltpu.with_memory_space_constraint(x, pltpu.VMEM) for x in operands]
    inside = pl.BlockSpec(memory_space=pltpu.VMEM)
    return pl.pallas_call(
        functools.partial(product_kernel, bool(crossed), len(own)),
        out_shape=[jax.ShapeDtypeStruct((rows // 2, width), dtype)] * 2,
        in_specs=[pl.BlockSpec(memory_space=pltpu.SMEM)] + [inside] * len(operands),
        out_specs=[inside, inside],
        compiler_params=pltpu.CompilerParams(vmem_limit_bytes=12 * 1024 * 1024),
        cost_estimate=cost,
    )(place, *operands)


def add_kernel(lows, mine_low_ref, mine_high_ref, *refs):
    half = mine_low_ref.shape[0]
    low, high = mine_low_ref[...], mine_high_ref[...]
    for i, ref in enumerate(refs[:-1]):
        if i < lows:
            low = low + ref[...].astype(jnp.float32)
        else:
            high = high + ref[...].astype(jnp.float32)
    refs[-1][:half] = low.astype(refs[-1].dtype)
    refs[-1][half:] = high.astype(refs[-1].dtype)


def add(mine, low, high):
    half, width = mine[0].shape
    inside = pl.BlockSpec(memory_space=pltpu.VMEM)
    return pl.pallas_call(
        functools.partial(add_kernel, len(low)),
        out_shape=jax.ShapeDtypeStruct((2 * half, width), jnp.bfloat16),
        in_specs=[inside] * (2 + len(low) + len(high)),
        out_specs=inside,
        compiler_params=pltpu.CompilerParams(vmem_limit_bytes=12 * 1024 * 1024),
        cost_estimate=FREE,
    )(*mine, *low, *high)


def hold(token, *arrays, flops=5 * 10**10):
    anywhere = pl.BlockSpec(memory_space=pl.ANY)
    return pl.pallas_call(
        lambda *refs: None,
        out_shape=jax.ShapeDtypeStruct(token.shape, token.dtype),
        in_specs=[anywhere] * (1 + len(arrays)),
        out_specs=anywhere,
        input_output_aliases={0: 0},
        compiler_params=pltpu.CompilerParams(vmem_limit_bytes=1024 * 1024),
        cost_estimate=pl.CostEstimate(flops=flops, bytes_accessed=0, transcendentals=0),
    )(token, *arrays)


def after(token, arrays):
    return lax.optimization_barrier((token, arrays))


def per_device(train_hidden, out_grad, master, first_moment, second_moment, decode_hidden):
    devices, planes = lax.axis_size("replica"), lax.axis_size("tensor")
    chips = devices // 2
    plane, device = lax.axis_index("tensor"), lax.axis_index("replica")
    chip, core = lax.div(device, 2), lax.rem(device, 2)
    parity = lax.rem(plane, 2)
    rows, hidden = decode_hidden.shape
    block = hidden // devices
    tokens, width = out_grad.shape[0], out_grad.shape[1] // planes
    token = jnp.stack([plane, core, chip]).astype(jnp.int32)

    near = 1
    sides = [mask for mask in range(2, chips) if mask % 2 == 0]
    fars = [mask for mask in range(2, chips) if mask % 2 == 1]

    def to_peer(array, mask, cross=0):
        return xor_permute(array, "replica", devices, 2 * mask + cross)

    windows = decode_hidden.T.reshape(devices, block, rows)

    def part(mask, to_core):
        return lax.dynamic_index_in_dim(windows, (chip ^ mask) * 2 + to_core, 0, keepdims=False)

    far_cuts, column_cuts = cut(token, windows, out_grad, planes, fars)
    shared = {mask: to_peer(piece, mask) for mask, piece in zip(fars, far_cuts, strict=True)}
    pieces = [xor_permute(piece, "tensor", planes, mask + 1) for mask, piece in enumerate(column_cuts)]
    token = hold(token, *far_cuts, *column_cuts)

    first = block * 5 // 8 // 16 * 16

    def straight_part(mask, low):
        return lax.dynamic_slice(windows, ((chip ^ mask) * 2, low, 0), (2, block - low, rows))

    token, (windows, train) = after(token, (windows, train_hidden.T))
    own_columns = lax.dynamic_slice(out_grad, (0, plane * width), (tokens, width))
    cuts = [*range(0, block, min(160, block)), block]
    middle = cuts[len(cuts) // 2] if len(cuts) > 2 else block
    trains = [train[:middle], train[middle:]]
    near_cut = part(near, core ^ parity)[:first]
    side_cuts = {mask: straight_part(mask, 0) for mask in sides}
    rest_cut = straight_part(near, first)
    shared[near] = to_peer(near_cut, near)
    straight = {mask: to_peer(piece, mask) for mask, piece in side_cuts.items()}
    token = hold(token, near_cut, rest_cut, *side_cuts.values(), *trains, own_columns)

    passed = {}
    for mask in fars:
        token, shared[mask] = after(token, shared[mask])
        passed[mask] = xor_permute(shared[mask], "tensor", planes, 1)
    token = hold(token, *(shared[mask] for mask in fars))

    token, (pieces, rest_cut) = after(token, (pieces, rest_cut))
    straight[near] = to_peer(rest_cut, near)
    swapped = [to_peer(piece, 0, 1) for piece in pieces]
    state = (master, first_moment, second_moment)
    def step(at, before):
        rows = [cut for cut in cuts if (cut <= middle if at == 0 else cut >= middle)]
        return list(adam(token, planes, trains[at], own_columns, pieces, swapped, state, rows, before))

    out = step(0, [])
    weights = [out[3]]
    shared[near], out[0] = lax.optimization_barrier((shared[near], out[0]))
    passed[near] = xor_permute(shared[near], "tensor", planes, 1)
    if middle < block:
        out = step(1, out[:3])
        weights.append(out[3])
    new_master, new_first, new_second = out[:3]

    other = [to_peer(array, 0, 1) for array in weights]
    token = hold(token, *(passed[mask] for mask in fars), flops=2 * 10**9)
    token = hold(token, passed[near], *straight.values(), flops=10**11)

    low = {near: [], **{mask: [] for mask in sides}}
    high = {near: [], **{mask: [] for mask in sides}}
    for mask in fars:
        out = product(token, (shared[mask], passed[mask]), (), weights, other, jnp.bfloat16, FREE)
        low[mask ^ near].append(to_peer(out[0], near))
        high[near].append(to_peer(out[1], mask ^ near))
    back = []
    for mask in (near, *sides):
        crossed = (shared[near], passed[near]) if mask == near else ()
        out = product(token, crossed, (straight[mask],), weights, other, jnp.float32, FREE)
        back.append(to_peer(add(out, low[mask], high[mask]), mask))
    cost = pl.CostEstimate(flops=4 * rows * block * width, bytes_accessed=4 * block * width, transcendentals=0)
    mine = lax.dynamic_slice(windows, (chip * 2, 0, 0), (2, block, rows))
    total = product(token, (), (mine,), weights, other, jnp.float32, cost)
    total = lax.optimization_barrier(jnp.concatenate(total, axis=0))
    for sums in back:
        total = total + sums.astype(jnp.float32)
    decoded = total.astype(jnp.bfloat16)
    return (new_master, new_first, new_second, decoded)


def solution(mesh):
    placed = (
        P(None, "replica"),
        P("tensor", None),
        P("replica", "tensor"),
        P("replica", "tensor"),
        P("replica", "tensor"),
        P("replica", None),
    )
    return jax.shard_map(
        per_device,
        mesh=mesh,
        in_specs=placed,
        out_specs=(
            P("replica", "tensor"),
            P("replica", "tensor"),
            P("replica", "tensor"),
            P("replica", "tensor"),
        ),
        check_vma=False,
    )
```

```python
import functools
import math

import jax
import jax.numpy as jnp
from jax import lax
from jax.experimental import pallas as pl
from jax.experimental.pallas import tpu as pltpu
from jax.sharding import PartitionSpec as P

FREE = pl.CostEstimate(flops=0, bytes_accessed=0, transcendentals=0)
OVER_FIRST = (((0,), (0,)), ((), ()))


def xor_permute(array, axis, size, mask):
    return lax.ppermute(array, axis, [(i, i ^ mask) for i in range(size)])


def cut_kernel(planes, masks, place_ref, windows_ref, out_grad_ref, *refs):
    *target_refs, sems = refs
    plane, core, chip = place_ref[0], place_ref[1], place_ref[2]
    half, width = target_refs[-1].shape
    copies = []
    for mask, target_ref in zip(masks, target_refs):
        device = (chip ^ mask) * 2 + (core ^ lax.rem(plane, 2))
        copies.append(pltpu.make_async_copy(windows_ref.at[device], target_ref, sems.at[len(copies)]))
    for mask, target_ref in zip(range(1, planes), target_refs[len(masks) :]):
        rows = pl.ds(pl.multiple_of(core * half, half), half)
        columns = pl.ds(pl.multiple_of((plane ^ mask) * width, width), width)
        copies.append(pltpu.make_async_copy(out_grad_ref.at[rows, columns], target_ref, sems.at[len(copies)]))
    for copy in copies:
        copy.start()
    for copy in copies:
        copy.wait()


def cut(place, windows, out_grad, planes, masks):
    tokens, width = out_grad.shape[0], out_grad.shape[1] // planes
    anywhere = pl.BlockSpec(memory_space=pl.ANY)
    pieces = len(masks) + planes - 1
    out = pl.pallas_call(
        functools.partial(cut_kernel, planes, masks),
        out_shape=[pltpu.VMEM(windows.shape[1:], windows.dtype)] * len(masks)
        + [pltpu.VMEM((tokens // 2, width), out_grad.dtype)] * (planes - 1),
        in_specs=[pl.BlockSpec(memory_space=pltpu.SMEM), anywhere, anywhere],
        out_specs=[pl.BlockSpec(memory_space=pltpu.VMEM)] * pieces,
        scratch_shapes=[pltpu.SemaphoreType.DMA((pieces,))],
        compiler_params=pltpu.CompilerParams(vmem_limit_bytes=8 * 1024 * 1024),
        cost_estimate=FREE,
    )(place, *[pltpu.with_memory_space_constraint(x, pltpu.HBM) for x in (windows, out_grad)])
    return out[: len(masks)], out[len(masks) :]


def adam_kernel(planes, scale, cuts, parts, waits, place_ref, own_ref, *refs):
    crossed = planes - 1
    fetched_refs, swapped_refs = refs[:crossed], refs[crossed : 2 * crossed]
    hidden_ref, *state_refs = refs[2 * crossed : 2 * crossed + 4]
    refs = refs[2 * crossed + 4 + waits :]
    out_refs, weights_refs = refs[:3], refs[3 : 3 + parts]
    columns_ref, rows_ref, held_ref, row_sem, in_sems, out_sems = refs[3 + parts :]
    base = cuts[0]
    rows_copy = pltpu.make_async_copy(hidden_ref, rows_ref, row_sem)
    copies_in, copies_out = [], []
    for i, (low, high) in enumerate(zip(cuts, cuts[1:])):
        here, there = slice(low - base, high - base), slice(low, high)
        copies_in.append(
            [
                pltpu.make_async_copy(ref.at[there], held_ref.at[k, here], in_sems.at[i, k])
                for k, ref in enumerate(state_refs)
            ]
        )
        copies_out.append(
            [
                pltpu.make_async_copy(held_ref.at[k, here], ref.at[there], out_sems.at[i, k])
                for k, ref in enumerate(out_refs)
            ]
        )
    rows_copy.start()
    for copies in copies_in[:2]:
        for copy in copies:
            copy.start()

    tokens = own_ref.shape[0]
    half = tokens // 2
    plane, core = place_ref[0], place_ref[1]
    columns_ref[pl.ds(pl.multiple_of(plane * tokens, tokens), tokens), :] = own_ref[...]
    for mask in range(1, planes):
        start = (plane ^ mask) * tokens
        mine = pl.multiple_of(start + core * half, half)
        other = pl.multiple_of(start + (1 - core) * half, half)
        columns_ref[pl.ds(mine, half), :] = fetched_refs[mask - 1][...]
        columns_ref[pl.ds(other, half), :] = swapped_refs[mask - 1][...]

    rows_copy.wait()
    for i, (low, high) in enumerate(zip(cuts, cuts[1:])):
        here = slice(low - base, high - base)
        grad = jnp.dot(rows_ref[here], columns_ref[...], preferred_element_type=jnp.float32)
        grad = grad * scale
        for copy in copies_in[i]:
            copy.wait()
        for copy in copies_in[i + 2] if i + 2 < len(copies_in) else ():
            copy.start()
        new_first = 0.9 * held_ref[1, here] + 0.1 * grad
        new_second = 0.95 * held_ref[2, here] + 0.05 * grad * grad
        new_master = held_ref[0, here] - 0.002 * new_first / (jnp.sqrt(new_second) + 1e-08)
        part, at = divmod(low - base, weights_refs[0].shape[0])
        weights_refs[part][at : at + high - low] = new_master.astype(jnp.bfloat16)
        for k, new in enumerate((new_master, new_first, new_second)):
            held_ref[k, here] = new
            copies_out[i][k].start()
    for copies in copies_out:
        for copy in copies:
            copy.wait()


def adam(place, planes, hidden, own, fetched, swapped, state, cuts, parts, before):
    count, tokens_all = hidden.shape
    rows, width = state[0].shape
    full = pltpu.HBM((rows, width), jnp.float32)
    inside = pl.BlockSpec(memory_space=pltpu.VMEM)
    outside = pl.BlockSpec(memory_space=pl.ANY)
    near = [own, *fetched, *swapped]
    far = [pltpu.with_memory_space_constraint(x, pltpu.HBM) for x in (hidden, *state, *before)]
    return pl.pallas_call(
        functools.partial(adam_kernel, planes, 1.0 / math.sqrt(tokens_all), cuts, parts, len(before)),
        out_shape=[full] * 3 + [jax.ShapeDtypeStruct((count // parts, width), jnp.bfloat16)] * parts,
        in_specs=[pl.BlockSpec(memory_space=pltpu.SMEM)] + [inside] * len(near) + [outside] * len(far),
        out_specs=[outside] * 3 + [inside] * parts,
        scratch_shapes=[
            pltpu.VMEM((tokens_all, width), jnp.bfloat16),
            pltpu.VMEM((count, tokens_all), jnp.bfloat16),
            pltpu.VMEM((3, count, width), jnp.float32),
            pltpu.SemaphoreType.DMA,
            pltpu.SemaphoreType.DMA((len(cuts) - 1, 3)),
            pltpu.SemaphoreType.DMA((len(cuts) - 1, 3)),
        ],
        input_output_aliases={1 + len(near) + 4 + i: i for i in range(len(before))},
        compiler_params=pltpu.CompilerParams(vmem_limit_bytes=28 * 1024 * 1024),
        cost_estimate=FREE,
    )(place, *near, *far)


def product_kernel(crossed, parts, place_ref, *refs):
    own_refs, other_refs, out_refs = refs[-2 * parts - 2 : -parts - 2], refs[-parts - 2 : -2], refs[-2:]
    held_refs = refs[: -2 * parts - 2]
    parity, core = lax.rem(place_ref[0], 2), place_ref[1]
    cut = held_refs[0].shape[0] if crossed else 0

    def dot(weights_refs, low, high, read):
        total, at = 0.0, 0
        for ref in weights_refs:
            begin, end = max(low, at), min(high, at + ref.shape[0])
            if begin < end:
                total = total + lax.dot_general(
                    read(begin, end), ref[begin - at : end - at], OVER_FIRST, preferred_element_type=jnp.float32
                )
            at += ref.shape[0]
        return total

    def write(first_refs, second_refs):
        block = sum(ref.shape[0] for ref in own_refs)
        total = 0.0
        if crossed:
            total = dot(first_refs, 0, cut, lambda begin, end: held_refs[0][begin:end])
            total = total + dot(second_refs, 0, cut, lambda begin, end: held_refs[1][begin:end])
        if cut < block:
            straight_ref = held_refs[-1]
            total = total + dot(own_refs, cut, block, lambda begin, end: straight_ref[core, begin - cut : end - cut])
            total = total + dot(
                other_refs, cut, block, lambda begin, end: straight_ref[1 - core, begin - cut : end - cut]
            )
        half = out_refs[0].shape[0]
        out_refs[0][...] = total[:half].astype(out_refs[0].dtype)
        out_refs[1][...] = total[half:].astype(out_refs[1].dtype)

    if crossed:
        pl.when(parity == 0)(lambda: write(own_refs, other_refs))
        pl.when(parity != 0)(lambda: write(other_refs, own_refs))
    else:
        write(own_refs, other_refs)


def product(place, crossed, straight, own, other, dtype, cost):
    width = own[0].shape[1]
    rows = (*crossed, *straight)[0].shape[-1]
    operands = [*crossed, *straight, *own, *other]
    operands = [pltpu.with_memory_space_constraint(x, pltpu.VMEM) for x in operands]
    inside = pl.BlockSpec(memory_space=pltpu.VMEM)
    return pl.pallas_call(
        functools.partial(product_kernel, bool(crossed), len(own)),
        out_shape=[jax.ShapeDtypeStruct((rows // 2, width), dtype)] * 2,
        in_specs=[pl.BlockSpec(memory_space=pltpu.SMEM)] + [inside] * len(operands),
        out_specs=[inside, inside],
        compiler_params=pltpu.CompilerParams(vmem_limit_bytes=12 * 1024 * 1024),
        cost_estimate=cost,
    )(place, *operands)


def products_kernel(count, parts, place_ref, *refs):
    held_refs, out_refs = refs[:count], refs[count + 2 * parts :]
    own_refs, other_refs = refs[count : count + parts], refs[count + parts : count + 2 * parts]
    core = place_ref[1]
    half = out_refs[0].shape[0]
    for first in range(0, count, 2):
        pair_refs = held_refs[first : first + 2]
        total = 0.0
        for weights_refs, of_core in ((own_refs, core), (other_refs, 1 - core)):
            at = 0
            for ref in weights_refs:
                rows = slice(at, at + ref.shape[0])
                held = jnp.concatenate([held_ref[of_core, rows] for held_ref in pair_refs], axis=1)
                total = total + lax.dot_general(held, ref[...], OVER_FIRST, preferred_element_type=jnp.float32)
                at += ref.shape[0]
        for i in range(2 * len(pair_refs)):
            out_refs[2 * first + i][...] = total[i * half : (i + 1) * half]


def products(place, held, own, other):
    width, rows = own[0].shape[1], held[0].shape[-1]
    operands = [pltpu.with_memory_space_constraint(x, pltpu.VMEM) for x in (*held, *own, *other)]
    inside = pl.BlockSpec(memory_space=pltpu.VMEM)
    out = pl.pallas_call(
        functools.partial(products_kernel, len(held), len(own)),
        out_shape=[jax.ShapeDtypeStruct((rows // 2, width), jnp.float32)] * (2 * len(held)),
        in_specs=[pl.BlockSpec(memory_space=pltpu.SMEM)] + [inside] * len(operands),
        out_specs=[inside] * (2 * len(held)),
        compiler_params=pltpu.CompilerParams(vmem_limit_bytes=20 * 1024 * 1024),
        cost_estimate=FREE,
    )(place, *operands)
    return [out[2 * i : 2 * i + 2] for i in range(len(held))]


def add_kernel(lows, mine_low_ref, mine_high_ref, *refs):
    half = mine_low_ref.shape[0]
    low, high = mine_low_ref[...], mine_high_ref[...]
    for i, ref in enumerate(refs[:-1]):
        if i < lows:
            low = low + ref[...].astype(jnp.float32)
        else:
            high = high + ref[...].astype(jnp.float32)
    refs[-1][:half] = low.astype(refs[-1].dtype)
    refs[-1][half:] = high.astype(refs[-1].dtype)


def add(mine, low, high):
    half, width = mine[0].shape
    inside = pl.BlockSpec(memory_space=pltpu.VMEM)
    return pl.pallas_call(
        functools.partial(add_kernel, len(low)),
        out_shape=jax.ShapeDtypeStruct((2 * half, width), jnp.bfloat16),
        in_specs=[inside] * (2 + len(low) + len(high)),
        out_specs=inside,
        compiler_params=pltpu.CompilerParams(vmem_limit_bytes=12 * 1024 * 1024),
        cost_estimate=FREE,
    )(*mine, *low, *high)


def hold(token, *arrays, flops=5 * 10**10):
    anywhere = pl.BlockSpec(memory_space=pl.ANY)
    return pl.pallas_call(
        lambda *refs: None,
        out_shape=jax.ShapeDtypeStruct(token.shape, token.dtype),
        in_specs=[anywhere] * (1 + len(arrays)),
        out_specs=anywhere,
        input_output_aliases={0: 0},
        compiler_params=pltpu.CompilerParams(vmem_limit_bytes=1024 * 1024),
        cost_estimate=pl.CostEstimate(flops=flops, bytes_accessed=0, transcendentals=0),
    )(token, *arrays)


def after(token, arrays):
    return lax.optimization_barrier((token, arrays))


def per_device(train_hidden, out_grad, master, first_moment, second_moment, decode_hidden):
    devices, planes = lax.axis_size("replica"), lax.axis_size("tensor")
    chips = devices // 2
    plane, device = lax.axis_index("tensor"), lax.axis_index("replica")
    chip, core = lax.div(device, 2), lax.rem(device, 2)
    parity = lax.rem(plane, 2)
    rows, hidden = decode_hidden.shape
    block = hidden // devices
    tokens, width = out_grad.shape[0], out_grad.shape[1] // planes
    token = jnp.stack([plane, core, chip]).astype(jnp.int32)

    near = 1
    sides = [mask for mask in range(2, chips) if mask % 2 == 0]
    fars = [mask for mask in range(2, chips) if mask % 2 == 1]

    def to_peer(array, mask, cross=0):
        return xor_permute(array, "replica", devices, 2 * mask + cross)

    windows = decode_hidden.T.reshape(devices, block, rows)

    def part(mask, to_core):
        return lax.dynamic_index_in_dim(windows, (chip ^ mask) * 2 + to_core, 0, keepdims=False)

    far_cuts, column_cuts = cut(token, windows, out_grad, planes, fars)
    shared = {mask: to_peer(piece, mask) for mask, piece in zip(fars, far_cuts, strict=True)}
    pieces = [xor_permute(piece, "tensor", planes, mask + 1) for mask, piece in enumerate(column_cuts)]
    token = hold(token, *far_cuts, *column_cuts)

    def both_parts(mask):
        return lax.dynamic_slice(windows, ((chip ^ mask) * 2, 0, 0), (2, block, rows))

    token, (windows, train) = after(token, (windows, train_hidden.T))
    own_columns = lax.dynamic_slice(out_grad, (0, plane * width), (tokens, width))
    cuts = [*range(0, block, min(160, block)), block]
    middle = cuts[len(cuts) * 2 // 3] if len(cuts) > 2 else block
    parts = 2 if middle % (2 * cuts[1]) == 0 else 1
    trains = [train[:middle], train[middle:]] if middle < block else [train]
    straight_cuts = {mask: both_parts(mask) for mask in (near, *sides)}
    straight = {mask: to_peer(piece, mask) for mask, piece in straight_cuts.items()}
    token = hold(token, *straight_cuts.values(), *trains, own_columns)

    passed = {}
    for mask in fars:
        token, shared[mask] = after(token, shared[mask])
        passed[mask] = xor_permute(shared[mask], "tensor", planes, 1)
    token = hold(token, *(shared[mask] for mask in fars))

    token, pieces = after(token, pieces)
    swapped = [to_peer(piece, 0, 1) for piece in pieces]
    state = (master, first_moment, second_moment)
    def step(at, before):
        rows = [cut for cut in cuts if (cut <= middle if at == 0 else cut >= middle)]
        return list(adam(token, planes, trains[at], own_columns, pieces, swapped, state, rows, parts if at == 0 else 1, before))

    out = step(0, [])
    weights = out[3:]
    if middle < block:
        out = step(1, out[:3])
        weights.append(out[3])
    new_master, new_first, new_second = out[:3]

    other = [to_peer(array, 0, 1) for array in weights]
    far_token = hold(token, *(passed[mask] for mask in fars), flops=8 * 10**9)
    token = hold(token, *straight.values(), flops=35 * 10**8)

    low = {near: [], **{mask: [] for mask in sides}}
    high = {near: [], **{mask: [] for mask in sides}}
    for mask in fars:
        out = product(far_token, (shared[mask], passed[mask]), (), weights, other, jnp.bfloat16, FREE)
        low[mask ^ near].append(to_peer(out[0], near))
        high[near].append(to_peer(out[1], mask ^ near))
    back = []
    order = (near, *sides)
    outs = []
    for at in range(0, len(order), 2):
        outs += products(token, [straight[mask] for mask in order[at : at + 2]], weights, other)
    for mask, out in zip(order, outs, strict=True):
        back.append(to_peer(add(out, low[mask], high[mask]), mask))
    cost = pl.CostEstimate(flops=4 * rows * block * width, bytes_accessed=4 * block * width, transcendentals=0)
    total = product(token, (), (both_parts(0),), weights, other, jnp.float32, cost)
    total = lax.optimization_barrier(jnp.concatenate(total, axis=0))
    for sums in back:
        total = total + sums.astype(jnp.float32)
    decoded = total.astype(jnp.bfloat16)
    return (new_master, new_first, new_second, decoded)


def solution(mesh):
    placed = (
        P(None, "replica"),
        P("tensor", None),
        P("replica", "tensor"),
        P("replica", "tensor"),
        P("replica", "tensor"),
        P("replica", None),
    )
    return jax.shard_map(
        per_device,
        mesh=mesh,
        in_specs=placed,
        out_specs=(
            P("replica", "tensor"),
            P("replica", "tensor"),
            P("replica", "tensor"),
            P("replica", "tensor"),
        ),
        check_vma=False,
    )
```

```python
import functools
import math

import jax
import jax.numpy as jnp
from jax import lax
from jax.experimental import pallas as pl
from jax.experimental.pallas import tpu as pltpu
from jax.sharding import PartitionSpec as P

FREE = pl.CostEstimate(flops=0, bytes_accessed=0, transcendentals=0)
OVER_FIRST = (((0,), (0,)), ((), ()))


def xor_permute(array, axis, size, mask):
    return lax.ppermute(array, axis, [(i, i ^ mask) for i in range(size)])


def cut_kernel(planes, masks, place_ref, windows_ref, out_grad_ref, *refs):
    *target_refs, sems = refs
    plane, core, chip = place_ref[0], place_ref[1], place_ref[2]
    half, width = target_refs[-1].shape
    copies = []
    for mask, target_ref in zip(masks, target_refs):
        device = (chip ^ mask) * 2 + (core ^ lax.rem(plane, 2))
        copies.append(pltpu.make_async_copy(windows_ref.at[device], target_ref, sems.at[len(copies)]))
    for mask, target_ref in zip(range(1, planes), target_refs[len(masks) :]):
        rows = pl.ds(pl.multiple_of(core * half, half), half)
        columns = pl.ds(pl.multiple_of((plane ^ mask) * width, width), width)
        copies.append(pltpu.make_async_copy(out_grad_ref.at[rows, columns], target_ref, sems.at[len(copies)]))
    for copy in copies:
        copy.start()
    for copy in copies:
        copy.wait()


def cut(place, windows, out_grad, planes, masks):
    tokens, width = out_grad.shape[0], out_grad.shape[1] // planes
    anywhere = pl.BlockSpec(memory_space=pl.ANY)
    pieces = len(masks) + planes - 1
    out = pl.pallas_call(
        functools.partial(cut_kernel, planes, masks),
        out_shape=[pltpu.VMEM(windows.shape[1:], windows.dtype)] * len(masks)
        + [pltpu.VMEM((tokens // 2, width), out_grad.dtype)] * (planes - 1),
        in_specs=[pl.BlockSpec(memory_space=pltpu.SMEM), anywhere, anywhere],
        out_specs=[pl.BlockSpec(memory_space=pltpu.VMEM)] * pieces,
        scratch_shapes=[pltpu.SemaphoreType.DMA((pieces,))],
        compiler_params=pltpu.CompilerParams(vmem_limit_bytes=8 * 1024 * 1024),
        cost_estimate=FREE,
    )(place, *[pltpu.with_memory_space_constraint(x, pltpu.HBM) for x in (windows, out_grad)])
    return out[: len(masks)], out[len(masks) :]


def adam_kernel(planes, scale, cuts, parts, waits, place_ref, own_ref, *refs):
    crossed = planes - 1
    fetched_refs, swapped_refs = refs[:crossed], refs[crossed : 2 * crossed]
    hidden_ref, *state_refs = refs[2 * crossed : 2 * crossed + 4]
    refs = refs[2 * crossed + 4 + waits :]
    out_refs, weights_refs = refs[:3], refs[3 : 3 + parts]
    columns_ref, rows_ref, held_ref, row_sem, in_sems, out_sems = refs[3 + parts :]
    base = cuts[0]
    rows_copy = pltpu.make_async_copy(hidden_ref, rows_ref, row_sem)
    copies_in, copies_out = [], []
    for i, (low, high) in enumerate(zip(cuts, cuts[1:])):
        here, there = slice(low - base, high - base), slice(low, high)
        copies_in.append(
            [
                pltpu.make_async_copy(ref.at[there], held_ref.at[k, here], in_sems.at[i, k])
                for k, ref in enumerate(state_refs)
            ]
        )
        copies_out.append(
            [
                pltpu.make_async_copy(held_ref.at[k, here], ref.at[there], out_sems.at[i, k])
                for k, ref in enumerate(out_refs)
            ]
        )
    rows_copy.start()
    for copies in copies_in[:2]:
        for copy in copies:
            copy.start()

    tokens = own_ref.shape[0]
    half = tokens // 2
    plane, core = place_ref[0], place_ref[1]
    columns_ref[pl.ds(pl.multiple_of(plane * tokens, tokens), tokens), :] = own_ref[...]
    for mask in range(1, planes):
        start = (plane ^ mask) * tokens
        mine = pl.multiple_of(start + core * half, half)
        other = pl.multiple_of(start + (1 - core) * half, half)
        columns_ref[pl.ds(mine, half), :] = fetched_refs[mask - 1][...]
        columns_ref[pl.ds(other, half), :] = swapped_refs[mask - 1][...]

    rows_copy.wait()
    for i, (low, high) in enumerate(zip(cuts, cuts[1:])):
        here = slice(low - base, high - base)
        grad = jnp.dot(rows_ref[here], columns_ref[...], preferred_element_type=jnp.float32)
        grad = grad * scale
        for copy in copies_in[i]:
            copy.wait()
        for copy in copies_in[i + 2] if i + 2 < len(copies_in) else ():
            copy.start()
        new_first = 0.9 * held_ref[1, here] + 0.1 * grad
        new_second = 0.95 * held_ref[2, here] + 0.05 * grad * grad
        new_master = held_ref[0, here] - 0.002 * new_first / (jnp.sqrt(new_second) + 1e-08)
        part, at = divmod(low - base, weights_refs[0].shape[0])
        weights_refs[part][at : at + high - low] = new_master.astype(jnp.bfloat16)
        for k, new in enumerate((new_master, new_first, new_second)):
            held_ref[k, here] = new
            copies_out[i][k].start()
    for copies in copies_out:
        for copy in copies:
            copy.wait()


def adam(place, planes, hidden, own, fetched, swapped, state, cuts, parts, before):
    count, tokens_all = hidden.shape
    rows, width = state[0].shape
    full = pltpu.HBM((rows, width), jnp.float32)
    inside = pl.BlockSpec(memory_space=pltpu.VMEM)
    outside = pl.BlockSpec(memory_space=pl.ANY)
    near = [own, *fetched, *swapped]
    far = [pltpu.with_memory_space_constraint(x, pltpu.HBM) for x in (hidden, *state, *before)]
    return pl.pallas_call(
        functools.partial(adam_kernel, planes, 1.0 / math.sqrt(tokens_all), cuts, parts, len(before)),
        out_shape=[full] * 3 + [jax.ShapeDtypeStruct((count // parts, width), jnp.bfloat16)] * parts,
        in_specs=[pl.BlockSpec(memory_space=pltpu.SMEM)] + [inside] * len(near) + [outside] * len(far),
        out_specs=[outside] * 3 + [inside] * parts,
        scratch_shapes=[
            pltpu.VMEM((tokens_all, width), jnp.bfloat16),
            pltpu.VMEM((count, tokens_all), jnp.bfloat16),
            pltpu.VMEM((3, count, width), jnp.float32),
            pltpu.SemaphoreType.DMA,
            pltpu.SemaphoreType.DMA((len(cuts) - 1, 3)),
            pltpu.SemaphoreType.DMA((len(cuts) - 1, 3)),
        ],
        input_output_aliases={1 + len(near) + 4 + i: i for i in range(len(before))},
        compiler_params=pltpu.CompilerParams(vmem_limit_bytes=28 * 1024 * 1024),
        cost_estimate=FREE,
    )(place, *near, *far)


def product_kernel(crossed, parts, place_ref, *refs):
    own_refs, other_refs, out_refs = refs[-2 * parts - 2 : -parts - 2], refs[-parts - 2 : -2], refs[-2:]
    held_refs = refs[: -2 * parts - 2]
    parity, core = lax.rem(place_ref[0], 2), place_ref[1]
    cut = held_refs[0].shape[0] if crossed else 0

    def dot(weights_refs, low, high, read):
        total, at = 0.0, 0
        for ref in weights_refs:
            begin, end = max(low, at), min(high, at + ref.shape[0])
            if begin < end:
                total = total + lax.dot_general(
                    read(begin, end), ref[begin - at : end - at], OVER_FIRST, preferred_element_type=jnp.float32
                )
            at += ref.shape[0]
        return total

    def write(first_refs, second_refs):
        block = sum(ref.shape[0] for ref in own_refs)
        total = 0.0
        if crossed:
            total = dot(first_refs, 0, cut, lambda begin, end: held_refs[0][begin:end])
            total = total + dot(second_refs, 0, cut, lambda begin, end: held_refs[1][begin:end])
        if cut < block:
            straight_ref = held_refs[-1]
            total = total + dot(own_refs, cut, block, lambda begin, end: straight_ref[core, begin - cut : end - cut])
            total = total + dot(
                other_refs, cut, block, lambda begin, end: straight_ref[1 - core, begin - cut : end - cut]
            )
        half = out_refs[0].shape[0]
        out_refs[0][...] = total[:half].astype(out_refs[0].dtype)
        out_refs[1][...] = total[half:].astype(out_refs[1].dtype)

    if crossed:
        pl.when(parity == 0)(lambda: write(own_refs, other_refs))
        pl.when(parity != 0)(lambda: write(other_refs, own_refs))
    else:
        write(own_refs, other_refs)


def product(place, crossed, straight, own, other, dtype, cost):
    width = own[0].shape[1]
    rows = (*crossed, *straight)[0].shape[-1]
    operands = [*crossed, *straight, *own, *other]
    operands = [pltpu.with_memory_space_constraint(x, pltpu.VMEM) for x in operands]
    inside = pl.BlockSpec(memory_space=pltpu.VMEM)
    return pl.pallas_call(
        functools.partial(product_kernel, bool(crossed), len(own)),
        out_shape=[jax.ShapeDtypeStruct((rows // 2, width), dtype)] * 2,
        in_specs=[pl.BlockSpec(memory_space=pltpu.SMEM)] + [inside] * len(operands),
        out_specs=[inside, inside],
        compiler_params=pltpu.CompilerParams(vmem_limit_bytes=12 * 1024 * 1024),
        cost_estimate=cost,
    )(place, *operands)


def products_kernel(count, parts, place_ref, *refs):
    held_refs, out_refs = refs[:count], refs[count + 2 * parts :]
    own_refs, other_refs = refs[count : count + parts], refs[count + parts : count + 2 * parts]
    core = place_ref[1]
    half = out_refs[0].shape[0]
    for first in range(0, count, 2):
        pair_refs = held_refs[first : first + 2]
        total = 0.0
        for weights_refs, of_core in ((own_refs, core), (other_refs, 1 - core)):
            at = 0
            for ref in weights_refs:
                rows = slice(at, at + ref.shape[0])
                held = jnp.concatenate([held_ref[of_core, rows] for held_ref in pair_refs], axis=1)
                total = total + lax.dot_general(held, ref[...], OVER_FIRST, preferred_element_type=jnp.float32)
                at += ref.shape[0]
        for i in range(2 * len(pair_refs)):
            out_refs[2 * first + i][...] = total[i * half : (i + 1) * half]


def products(place, held, own, other):
    width, rows = own[0].shape[1], held[0].shape[-1]
    operands = [pltpu.with_memory_space_constraint(x, pltpu.VMEM) for x in (*held, *own, *other)]
    inside = pl.BlockSpec(memory_space=pltpu.VMEM)
    out = pl.pallas_call(
        functools.partial(products_kernel, len(held), len(own)),
        out_shape=[jax.ShapeDtypeStruct((rows // 2, width), jnp.float32)] * (2 * len(held)),
        in_specs=[pl.BlockSpec(memory_space=pltpu.SMEM)] + [inside] * len(operands),
        out_specs=[inside] * (2 * len(held)),
        compiler_params=pltpu.CompilerParams(vmem_limit_bytes=20 * 1024 * 1024),
        cost_estimate=FREE,
    )(place, *operands)
    return [out[2 * i : 2 * i + 2] for i in range(len(held))]


def add_kernel(lows, mine_low_ref, mine_high_ref, *refs):
    half = mine_low_ref.shape[0]
    low, high = mine_low_ref[...], mine_high_ref[...]
    for i, ref in enumerate(refs[:-1]):
        if i < lows:
            low = low + ref[...].astype(jnp.float32)
        else:
            high = high + ref[...].astype(jnp.float32)
    refs[-1][:half] = low.astype(refs[-1].dtype)
    refs[-1][half:] = high.astype(refs[-1].dtype)


def add(mine, low, high):
    half, width = mine[0].shape
    inside = pl.BlockSpec(memory_space=pltpu.VMEM)
    return pl.pallas_call(
        functools.partial(add_kernel, len(low)),
        out_shape=jax.ShapeDtypeStruct((2 * half, width), jnp.bfloat16),
        in_specs=[inside] * (2 + len(low) + len(high)),
        out_specs=inside,
        compiler_params=pltpu.CompilerParams(vmem_limit_bytes=12 * 1024 * 1024),
        cost_estimate=FREE,
    )(*mine, *low, *high)


def hold(token, *arrays, flops=5 * 10**10):
    anywhere = pl.BlockSpec(memory_space=pl.ANY)
    return pl.pallas_call(
        lambda *refs: None,
        out_shape=jax.ShapeDtypeStruct(token.shape, token.dtype),
        in_specs=[anywhere] * (1 + len(arrays)),
        out_specs=anywhere,
        input_output_aliases={0: 0},
        compiler_params=pltpu.CompilerParams(vmem_limit_bytes=1024 * 1024),
        cost_estimate=pl.CostEstimate(flops=flops, bytes_accessed=0, transcendentals=0),
    )(token, *arrays)


def after(token, arrays):
    return lax.optimization_barrier((token, arrays))


def per_device(train_hidden, out_grad, master, first_moment, second_moment, decode_hidden):
    devices, planes = lax.axis_size("replica"), lax.axis_size("tensor")
    chips = devices // 2
    plane, device = lax.axis_index("tensor"), lax.axis_index("replica")
    chip, core = lax.div(device, 2), lax.rem(device, 2)
    parity = lax.rem(plane, 2)
    rows, hidden = decode_hidden.shape
    block = hidden // devices
    tokens, width = out_grad.shape[0], out_grad.shape[1] // planes
    token = jnp.stack([plane, core, chip]).astype(jnp.int32)

    near = 1
    sides = [mask for mask in range(2, chips) if mask % 2 == 0]
    fars = [mask for mask in range(2, chips) if mask % 2 == 1]

    def to_peer(array, mask, cross=0):
        return xor_permute(array, "replica", devices, 2 * mask + cross)

    windows = decode_hidden.T.reshape(devices, block, rows)

    def part(mask, to_core):
        return lax.dynamic_index_in_dim(windows, (chip ^ mask) * 2 + to_core, 0, keepdims=False)

    far_cuts, column_cuts = cut(token, windows, out_grad, planes, fars)
    shared = {mask: to_peer(piece, mask) for mask, piece in zip(fars, far_cuts, strict=True)}
    pieces = [xor_permute(piece, "tensor", planes, mask + 1) for mask, piece in enumerate(column_cuts)]
    token = hold(token, *far_cuts, *column_cuts)

    def both_parts(mask):
        return lax.dynamic_slice(windows, ((chip ^ mask) * 2, 0, 0), (2, block, rows))

    token, (windows, train) = after(token, (windows, train_hidden.T))
    own_columns = lax.dynamic_slice(out_grad, (0, plane * width), (tokens, width))
    cuts = [*range(0, block, min(160, block)), block]
    middle = cuts[len(cuts) * 2 // 3] if len(cuts) > 2 else block
    parts = 2 if middle % (2 * cuts[1]) == 0 else 1
    trains = [train[:middle], train[middle:]] if middle < block else [train]
    straight_cuts = {mask: both_parts(mask) for mask in (near, *sides)}
    straight = {mask: to_peer(piece, mask) for mask, piece in straight_cuts.items()}
    token = hold(token, *straight_cuts.values(), *trains, own_columns)

    passed = {}
    for mask in fars:
        token, shared[mask] = after(token, shared[mask])
        passed[mask] = xor_permute(shared[mask], "tensor", planes, 1)
    token = hold(token, *(shared[mask] for mask in fars))

    token, pieces[-1] = after(token, pieces[-1])
    swapped = [to_peer(piece, 0, 1) for piece in pieces]
    state = (master, first_moment, second_moment)
    def step(at, before):
        rows = [cut for cut in cuts if (cut <= middle if at == 0 else cut >= middle)]
        return list(adam(token, planes, trains[at], own_columns, pieces, swapped, state, rows, parts if at == 0 else 1, before))

    out = step(0, [])
    weights = out[3:]
    if middle < block:
        out = step(1, out[:3])
        weights.append(out[3])
    new_master, new_first, new_second = out[:3]

    other = [to_peer(array, 0, 1) for array in weights]
    far_token = hold(token, *(passed[mask] for mask in fars), flops=8 * 10**9)
    token = hold(token, *straight.values(), flops=35 * 10**8)

    low = {near: [], **{mask: [] for mask in sides}}
    high = {near: [], **{mask: [] for mask in sides}}
    for mask in fars:
        out = product(far_token, (shared[mask], passed[mask]), (), weights, other, jnp.bfloat16, FREE)
        low[mask ^ near].append(to_peer(out[0], near))
        high[near].append(to_peer(out[1], mask ^ near))
    back = []
    order = (near, *sides)
    outs = []
    for at in range(0, len(order), 2):
        outs += products(token, [straight[mask] for mask in order[at : at + 2]], weights, other)
    for mask, out in zip(order, outs, strict=True):
        back.append(to_peer(add(out, low[mask], high[mask]), mask))
    cost = pl.CostEstimate(flops=4 * rows * block * width, bytes_accessed=4 * block * width, transcendentals=0)
    total = product(token, (), (both_parts(0),), weights, other, jnp.float32, cost)
    total = lax.optimization_barrier(jnp.concatenate(total, axis=0))
    for sums in back:
        total = total + sums.astype(jnp.float32)
    decoded = total.astype(jnp.bfloat16)
    return (new_master, new_first, new_second, decoded)


def solution(mesh):
    placed = (
        P(None, "replica"),
        P("tensor", None),
        P("replica", "tensor"),
        P("replica", "tensor"),
        P("replica", "tensor"),
        P("replica", None),
    )
    return jax.shard_map(
        per_device,
        mesh=mesh,
        in_specs=placed,
        out_specs=(
            P("replica", "tensor"),
            P("replica", "tensor"),
            P("replica", "tensor"),
            P("replica", "tensor"),
        ),
        check_vma=False,
    )
```

```python
import functools
import math

import jax
import jax.numpy as jnp
from jax import lax
from jax.experimental import pallas as pl
from jax.experimental.pallas import tpu as pltpu
from jax.sharding import PartitionSpec as P

FREE = pl.CostEstimate(flops=0, bytes_accessed=0, transcendentals=0)
OVER_FIRST = (((0,), (0,)), ((), ()))


def xor_permute(array, axis, size, mask):
    return lax.ppermute(array, axis, [(i, i ^ mask) for i in range(size)])


def cut_kernel(planes, masks, place_ref, windows_ref, out_grad_ref, *refs):
    *target_refs, sems = refs
    plane, core, chip = place_ref[0], place_ref[1], place_ref[2]
    half, width = target_refs[-1].shape
    copies = []
    for mask, target_ref in zip(masks, target_refs):
        device = (chip ^ mask) * 2 + (core ^ lax.rem(plane, 2))
        copies.append(pltpu.make_async_copy(windows_ref.at[device], target_ref, sems.at[len(copies)]))
    for mask, target_ref in zip(range(1, planes), target_refs[len(masks) :]):
        rows = pl.ds(pl.multiple_of(core * half, half), half)
        columns = pl.ds(pl.multiple_of((plane ^ mask) * width, width), width)
        copies.append(pltpu.make_async_copy(out_grad_ref.at[rows, columns], target_ref, sems.at[len(copies)]))
    for copy in copies:
        copy.start()
    for copy in copies:
        copy.wait()


def cut(place, windows, out_grad, planes, masks):
    tokens, width = out_grad.shape[0], out_grad.shape[1] // planes
    anywhere = pl.BlockSpec(memory_space=pl.ANY)
    pieces = len(masks) + planes - 1
    out = pl.pallas_call(
        functools.partial(cut_kernel, planes, masks),
        out_shape=[pltpu.VMEM(windows.shape[1:], windows.dtype)] * len(masks)
        + [pltpu.VMEM((tokens // 2, width), out_grad.dtype)] * (planes - 1),
        in_specs=[pl.BlockSpec(memory_space=pltpu.SMEM), anywhere, anywhere],
        out_specs=[pl.BlockSpec(memory_space=pltpu.VMEM)] * pieces,
        scratch_shapes=[pltpu.SemaphoreType.DMA((pieces,))],
        compiler_params=pltpu.CompilerParams(vmem_limit_bytes=8 * 1024 * 1024),
        cost_estimate=FREE,
    )(place, *[pltpu.with_memory_space_constraint(x, pltpu.HBM) for x in (windows, out_grad)])
    return out[: len(masks)], out[len(masks) :]


def adam_kernel(planes, scale, cuts, parts, waits, place_ref, own_ref, *refs):
    crossed = planes - 1
    fetched_refs, swapped_refs = refs[:crossed], refs[crossed : 2 * crossed]
    hidden_ref, *state_refs = refs[2 * crossed : 2 * crossed + 4]
    refs = refs[2 * crossed + 4 + waits :]
    out_refs, weights_refs = refs[:3], refs[3 : 3 + parts]
    columns_ref, rows_ref, held_ref, row_sem, in_sems, out_sems = refs[3 + parts :]
    base = cuts[0]
    rows_copy = pltpu.make_async_copy(hidden_ref, rows_ref, row_sem)
    copies_in, copies_out = [], []
    for i, (low, high) in enumerate(zip(cuts, cuts[1:])):
        here, there = slice(low - base, high - base), slice(low, high)
        copies_in.append(
            [
                pltpu.make_async_copy(ref.at[there], held_ref.at[k, here], in_sems.at[i, k])
                for k, ref in enumerate(state_refs)
            ]
        )
        copies_out.append(
            [
                pltpu.make_async_copy(held_ref.at[k, here], ref.at[there], out_sems.at[i, k])
                for k, ref in enumerate(out_refs)
            ]
        )
    rows_copy.start()
    for copies in copies_in[:2]:
        for copy in copies:
            copy.start()

    tokens = own_ref.shape[0]
    half = tokens // 2
    plane, core = place_ref[0], place_ref[1]
    columns_ref[pl.ds(pl.multiple_of(plane * tokens, tokens), tokens), :] = own_ref[...]
    for mask in range(1, planes):
        start = (plane ^ mask) * tokens
        mine = pl.multiple_of(start + core * half, half)
        other = pl.multiple_of(start + (1 - core) * half, half)
        columns_ref[pl.ds(mine, half), :] = fetched_refs[mask - 1][...]
        columns_ref[pl.ds(other, half), :] = swapped_refs[mask - 1][...]

    rows_copy.wait()
    for i, (low, high) in enumerate(zip(cuts, cuts[1:])):
        here = slice(low - base, high - base)
        grad = jnp.dot(rows_ref[here], columns_ref[...], preferred_element_type=jnp.float32)
        grad = grad * scale
        for copy in copies_in[i]:
            copy.wait()
        for copy in copies_in[i + 2] if i + 2 < len(copies_in) else ():
            copy.start()
        new_first = 0.9 * held_ref[1, here] + 0.1 * grad
        new_second = 0.95 * held_ref[2, here] + 0.05 * grad * grad
        new_master = held_ref[0, here] - 0.002 * new_first / (jnp.sqrt(new_second) + 1e-08)
        part, at = divmod(low - base, weights_refs[0].shape[0])
        weights_refs[part][at : at + high - low] = new_master.astype(jnp.bfloat16)
        for k, new in enumerate((new_master, new_first, new_second)):
            held_ref[k, here] = new
            copies_out[i][k].start()
    for copies in copies_out:
        for copy in copies:
            copy.wait()


def adam(place, planes, hidden, own, fetched, swapped, state, cuts, parts, before):
    count, tokens_all = hidden.shape
    rows, width = state[0].shape
    full = pltpu.HBM((rows, width), jnp.float32)
    inside = pl.BlockSpec(memory_space=pltpu.VMEM)
    outside = pl.BlockSpec(memory_space=pl.ANY)
    near = [own, *fetched, *swapped]
    far = [pltpu.with_memory_space_constraint(x, pltpu.HBM) for x in (hidden, *state, *before)]
    return pl.pallas_call(
        functools.partial(adam_kernel, planes, 1.0 / math.sqrt(tokens_all), cuts, parts, len(before)),
        out_shape=[full] * 3 + [jax.ShapeDtypeStruct((count // parts, width), jnp.bfloat16)] * parts,
        in_specs=[pl.BlockSpec(memory_space=pltpu.SMEM)] + [inside] * len(near) + [outside] * len(far),
        out_specs=[outside] * 3 + [inside] * parts,
        scratch_shapes=[
            pltpu.VMEM((tokens_all, width), jnp.bfloat16),
            pltpu.VMEM((count, tokens_all), jnp.bfloat16),
            pltpu.VMEM((3, count, width), jnp.float32),
            pltpu.SemaphoreType.DMA,
            pltpu.SemaphoreType.DMA((len(cuts) - 1, 3)),
            pltpu.SemaphoreType.DMA((len(cuts) - 1, 3)),
        ],
        input_output_aliases={1 + len(near) + 4 + i: i for i in range(len(before))},
        compiler_params=pltpu.CompilerParams(vmem_limit_bytes=28 * 1024 * 1024),
        cost_estimate=FREE,
    )(place, *near, *far)


def product_kernel(crossed, parts, place_ref, *refs):
    own_refs, other_refs, out_refs = refs[-2 * parts - 2 : -parts - 2], refs[-parts - 2 : -2], refs[-2:]
    held_refs = refs[: -2 * parts - 2]
    parity, core = lax.rem(place_ref[0], 2), place_ref[1]
    cut = held_refs[0].shape[0] if crossed else 0

    def dot(weights_refs, low, high, read):
        total, at = 0.0, 0
        for ref in weights_refs:
            begin, end = max(low, at), min(high, at + ref.shape[0])
            if begin < end:
                total = total + lax.dot_general(
                    read(begin, end), ref[begin - at : end - at], OVER_FIRST, preferred_element_type=jnp.float32
                )
            at += ref.shape[0]
        return total

    def write(first_refs, second_refs):
        block = sum(ref.shape[0] for ref in own_refs)
        total = 0.0
        if crossed:
            total = dot(first_refs, 0, cut, lambda begin, end: held_refs[0][begin:end])
            total = total + dot(second_refs, 0, cut, lambda begin, end: held_refs[1][begin:end])
        if cut < block:
            straight_ref = held_refs[-1]
            total = total + dot(own_refs, cut, block, lambda begin, end: straight_ref[core, begin - cut : end - cut])
            total = total + dot(
                other_refs, cut, block, lambda begin, end: straight_ref[1 - core, begin - cut : end - cut]
            )
        half = out_refs[0].shape[0]
        out_refs[0][...] = total[:half].astype(out_refs[0].dtype)
        out_refs[1][...] = total[half:].astype(out_refs[1].dtype)

    if crossed:
        pl.when(parity == 0)(lambda: write(own_refs, other_refs))
        pl.when(parity != 0)(lambda: write(other_refs, own_refs))
    else:
        write(own_refs, other_refs)


def product(place, crossed, straight, own, other, dtype, cost):
    width = own[0].shape[1]
    rows = (*crossed, *straight)[0].shape[-1]
    operands = [*crossed, *straight, *own, *other]
    operands = [pltpu.with_memory_space_constraint(x, pltpu.VMEM) for x in operands]
    inside = pl.BlockSpec(memory_space=pltpu.VMEM)
    return pl.pallas_call(
        functools.partial(product_kernel, bool(crossed), len(own)),
        out_shape=[jax.ShapeDtypeStruct((rows // 2, width), dtype)] * 2,
        in_specs=[pl.BlockSpec(memory_space=pltpu.SMEM)] + [inside] * len(operands),
        out_specs=[inside, inside],
        compiler_params=pltpu.CompilerParams(vmem_limit_bytes=12 * 1024 * 1024),
        cost_estimate=cost,
    )(place, *operands)


def products_kernel(count, parts, place_ref, *refs):
    held_refs, out_refs = refs[:count], refs[count + 2 * parts :]
    own_refs, other_refs = refs[count : count + parts], refs[count + parts : count + 2 * parts]
    core = place_ref[1]
    half = out_refs[0].shape[0]
    for first in range(0, count, 2):
        pair_refs = held_refs[first : first + 2]
        total = 0.0
        for weights_refs, of_core in ((own_refs, core), (other_refs, 1 - core)):
            blocks = [ref[...] for ref in weights_refs]
            if len(blocks) > 2:
                cut = blocks[0].shape[0] // 256 * 256
                blocks[1] = jnp.concatenate([weights_refs[0][cut:], blocks[1]], axis=0)
                blocks[0] = weights_refs[0][:cut]
            at = 0
            for block in blocks:
                rows = slice(at, at + block.shape[0])
                held = jnp.concatenate([held_ref[of_core, rows] for held_ref in pair_refs], axis=1)
                total = total + lax.dot_general(held, block, OVER_FIRST, preferred_element_type=jnp.float32)
                at += block.shape[0]
        for i in range(2 * len(pair_refs)):
            out_refs[2 * first + i][...] = total[i * half : (i + 1) * half]


def products(place, held, own, other):
    width, rows = own[0].shape[1], held[0].shape[-1]
    operands = [pltpu.with_memory_space_constraint(x, pltpu.VMEM) for x in (*held, *own, *other)]
    inside = pl.BlockSpec(memory_space=pltpu.VMEM)
    out = pl.pallas_call(
        functools.partial(products_kernel, len(held), len(own)),
        out_shape=[jax.ShapeDtypeStruct((rows // 2, width), jnp.float32)] * (2 * len(held)),
        in_specs=[pl.BlockSpec(memory_space=pltpu.SMEM)] + [inside] * len(operands),
        out_specs=[inside] * (2 * len(held)),
        compiler_params=pltpu.CompilerParams(vmem_limit_bytes=20 * 1024 * 1024),
        cost_estimate=FREE,
    )(place, *operands)
    return [out[2 * i : 2 * i + 2] for i in range(len(held))]


def add_kernel(lows, mine_low_ref, mine_high_ref, *refs):
    half = mine_low_ref.shape[0]
    low, high = mine_low_ref[...], mine_high_ref[...]
    for i, ref in enumerate(refs[:-1]):
        if i < lows:
            low = low + ref[...].astype(jnp.float32)
        else:
            high = high + ref[...].astype(jnp.float32)
    refs[-1][:half] = low.astype(refs[-1].dtype)
    refs[-1][half:] = high.astype(refs[-1].dtype)


def add(mine, low, high):
    half, width = mine[0].shape
    inside = pl.BlockSpec(memory_space=pltpu.VMEM)
    return pl.pallas_call(
        functools.partial(add_kernel, len(low)),
        out_shape=jax.ShapeDtypeStruct((2 * half, width), jnp.bfloat16),
        in_specs=[inside] * (2 + len(low) + len(high)),
        out_specs=inside,
        compiler_params=pltpu.CompilerParams(vmem_limit_bytes=12 * 1024 * 1024),
        cost_estimate=FREE,
    )(*mine, *low, *high)


def hold(token, *arrays, flops=5 * 10**10):
    anywhere = pl.BlockSpec(memory_space=pl.ANY)
    return pl.pallas_call(
        lambda *refs: None,
        out_shape=jax.ShapeDtypeStruct(token.shape, token.dtype),
        in_specs=[anywhere] * (1 + len(arrays)),
        out_specs=anywhere,
        input_output_aliases={0: 0},
        compiler_params=pltpu.CompilerParams(vmem_limit_bytes=1024 * 1024),
        cost_estimate=pl.CostEstimate(flops=flops, bytes_accessed=0, transcendentals=0),
    )(token, *arrays)


def after(token, arrays):
    return lax.optimization_barrier((token, arrays))


def per_device(train_hidden, out_grad, master, first_moment, second_moment, decode_hidden):
    devices, planes = lax.axis_size("replica"), lax.axis_size("tensor")
    chips = devices // 2
    plane, device = lax.axis_index("tensor"), lax.axis_index("replica")
    chip, core = lax.div(device, 2), lax.rem(device, 2)
    parity = lax.rem(plane, 2)
    rows, hidden = decode_hidden.shape
    block = hidden // devices
    tokens, width = out_grad.shape[0], out_grad.shape[1] // planes
    token = jnp.stack([plane, core, chip]).astype(jnp.int32)

    near = 1
    sides = [mask for mask in range(2, chips) if mask % 2 == 0]
    fars = [mask for mask in range(2, chips) if mask % 2 == 1]

    def to_peer(array, mask, cross=0):
        return xor_permute(array, "replica", devices, 2 * mask + cross)

    windows = decode_hidden.T.reshape(devices, block, rows)

    def part(mask, to_core):
        return lax.dynamic_index_in_dim(windows, (chip ^ mask) * 2 + to_core, 0, keepdims=False)

    far_cuts, column_cuts = cut(token, windows, out_grad, planes, fars)
    shared = {mask: to_peer(piece, mask) for mask, piece in zip(fars, far_cuts, strict=True)}
    pieces = [xor_permute(piece, "tensor", planes, mask + 1) for mask, piece in enumerate(column_cuts)]
    token = hold(token, *far_cuts, *column_cuts)

    def both_parts(mask):
        return lax.dynamic_slice(windows, ((chip ^ mask) * 2, 0, 0), (2, block, rows))

    token, (windows, train) = after(token, (windows, train_hidden.T))
    own_columns = lax.dynamic_slice(out_grad, (0, plane * width), (tokens, width))
    cuts = [*range(0, block, min(160, block)), block]
    middle = cuts[len(cuts) * 2 // 3] if len(cuts) > 2 else block
    parts = 2 if middle % (2 * cuts[1]) == 0 else 1
    trains = [train[:middle], train[middle:]] if middle < block else [train]
    straight_cuts = {mask: both_parts(mask) for mask in (near, *sides)}
    straight = {mask: to_peer(piece, mask) for mask, piece in straight_cuts.items()}
    token = hold(token, *straight_cuts.values(), *trains, own_columns)

    passed = {}
    for mask in fars:
        token, shared[mask] = after(token, shared[mask])
        passed[mask] = xor_permute(shared[mask], "tensor", planes, 1)
    token = hold(token, *(shared[mask] for mask in fars))

    token, pieces[-1] = after(token, pieces[-1])
    swapped = [to_peer(piece, 0, 1) for piece in pieces]
    state = (master, first_moment, second_moment)
    def step(at, before):
        rows = [cut for cut in cuts if (cut <= middle if at == 0 else cut >= middle)]
        return list(adam(token, planes, trains[at], own_columns, pieces, swapped, state, rows, parts if at == 0 else 1, before))

    out = step(0, [])
    weights = out[3:]
    if middle < block:
        out = step(1, out[:3])
        weights.append(out[3])
    new_master, new_first, new_second = out[:3]

    other = [to_peer(array, 0, 1) for array in weights]
    far_token = hold(token, *(passed[mask] for mask in fars), flops=8 * 10**9)
    token = hold(token, *straight.values(), flops=35 * 10**8)

    low = {near: [], **{mask: [] for mask in sides}}
    high = {near: [], **{mask: [] for mask in sides}}
    for mask in fars:
        out = product(far_token, (shared[mask], passed[mask]), (), weights, other, jnp.bfloat16, FREE)
        low[mask ^ near].append(to_peer(out[0], near))
        high[near].append(to_peer(out[1], mask ^ near))
    back = []
    order = (near, *sides)
    outs = []
    for at in range(0, len(order), 2):
        outs += products(token, [straight[mask] for mask in order[at : at + 2]], weights, other)
    for mask, out in zip(order, outs, strict=True):
        back.append(to_peer(add(out, low[mask], high[mask]), mask))
    cost = pl.CostEstimate(flops=4 * rows * block * width, bytes_accessed=4 * block * width, transcendentals=0)
    total = product(token, (), (both_parts(0),), weights, other, jnp.float32, cost)
    total = lax.optimization_barrier(jnp.concatenate(total, axis=0))
    for sums in back:
        total = total + sums.astype(jnp.float32)
    decoded = total.astype(jnp.bfloat16)
    return (new_master, new_first, new_second, decoded)


def solution(mesh):
    placed = (
        P(None, "replica"),
        P("tensor", None),
        P("replica", "tensor"),
        P("replica", "tensor"),
        P("replica", "tensor"),
        P("replica", None),
    )
    return jax.shard_map(
        per_device,
        mesh=mesh,
        in_specs=placed,
        out_specs=(
            P("replica", "tensor"),
            P("replica", "tensor"),
            P("replica", "tensor"),
            P("replica", "tensor"),
        ),
        check_vma=False,
    )
```
